32 devices in a mesh: row: 4 (over y, x), col: 8 (over z, core).
Axes of the slice: x: 2, y: 2, z: 4, core: 2. Of those that a mesh axis runs over, the one named last changes fastest.
Arguments:
- affinity: bfloat16 [4, 8, 16, 256, 256], P('row', 'col'), may hold values from 9e-05 to 32.4
- block_rows: int32 [4, 8, 16], P('row', 'col'), may hold values from 0 to 3, as said below
- block_cols: int32 [4, 8, 16], P('row', 'col'), may hold values from 0 to 7
- block_count: int32 [4, 8], P('row', 'col'), may hold values from 4 to 16, as said below
- labels: float32 [8192, 1024], P(('row', 'col')), may hold values from 0 to 1
- labelled: int32 [8192], P(('row', 'col')), may hold values 0 or 1
Outputs:
- scores: float32 [8192, 1024], P(('row', 'col'))
The draws below stay inside these ranges and needn't reach their ends.
Inputs may be any that keep to these rules, and one draw needn't show every extreme that they name: Within one entry (r, c) the pairs (block_rows, block_cols) of all 16 slots are distinct, and its first 4 slots name every row block once. `block_count`: some entry has all 16 slots live.
All inputs are finite; a program needn't handle non-finite values. No bound on the sum of `labelled` on one device may be relied on, other than what follows from the above.
Results may differ from the reference program's by a relative error of at most 0.0003.
Values may be sent and summed in bfloat16 or wider, within the bound.
No kernel may reach another device: no remote copies, remote signals or barrier semaphores. Data moves between devices by JAX's collectives and lax.ppermute only.
A program may use at most 128 MiB of HBM per device.

```python
import jax
import jax.numpy as jnp
from jax import lax

CLASSES = 1024
BS = 256
SWEEPS = 2
PROW = 4
PCOL = 8
MAXB = 16
NODES = 8192


def slot_layout(key):
    first_key, second_key = jax.random.split(jax.random.fold_in(key, 7))
    row_keys = jax.random.split(first_key, PROW * PCOL)
    row_perm = jax.vmap(lambda k: jax.random.permutation(k, PROW))(row_keys).reshape(PROW, PCOL, PROW)
    slot_index = jnp.arange(MAXB)
    local_row = slot_index % PROW
    slot_round = slot_index // PROW
    row_ids = jnp.take(row_perm, local_row, axis=2)
    col_keys = jax.random.split(second_key, PROW * PCOL * PROW)
    col_perm = jax.vmap(lambda k: jax.random.permutation(k, PCOL))(col_keys).reshape(PROW, PCOL, PROW, PCOL)
    picked = jnp.take_along_axis(col_perm, jnp.broadcast_to(row_ids[:, :, :, None], (PROW, PCOL, MAXB, 1)), axis=2)
    picked = picked.reshape(PROW, PCOL, MAXB, PCOL)
    round_index = jnp.broadcast_to(slot_round[None, None, :, None], (PROW, PCOL, MAXB, 1))
    col_ids = jnp.take_along_axis(picked, round_index, axis=3)[..., 0]
    return (row_ids.astype(jnp.int32), col_ids.astype(jnp.int32))


def cluster_total():
    return max(4, NODES // 512)


def node_clusters(key):
    return jax.random.randint(jax.random.fold_in(key, 13), (NODES,), 0, cluster_total()).astype(jnp.int32)


def draw_block_rows(key, part):
    return slot_layout(key)[0]


def draw_block_cols(key, part):
    return slot_layout(key)[1]


def draw_block_count(key, part):
    count_key, pick_key = jax.random.split(jax.random.fold_in(key, 11))
    counts = jax.random.randint(count_key, (PROW * PCOL,), PROW, MAXB + 1)
    chosen = jax.random.randint(pick_key, (), 0, PROW * PCOL)
    counts = jnp.where(jnp.arange(PROW * PCOL) == chosen, MAXB, counts)
    return counts.reshape(PROW, PCOL).astype(jnp.int32)


def draw_affinity(key, part):
    row_ids, col_ids = slot_layout(key)
    cluster_grid = node_clusters(key).reshape(PROW, PCOL, BS)
    grid_cols = jnp.broadcast_to(jnp.arange(PCOL)[None, :, None], row_ids.shape)
    grid_rows = jnp.broadcast_to(jnp.arange(PROW)[:, None, None], col_ids.shape)
    row_cluster = cluster_grid[row_ids, grid_cols]
    col_cluster = cluster_grid[grid_rows, col_ids]
    same = row_cluster[..., :, None] == col_cluster[..., None, :]
    mask_key, value_key = jax.random.split(jax.random.fold_in(key, 17), 2)
    pair_table = jax.random.uniform(jax.random.fold_in(key, 23), (cluster_total(), cluster_total()), jnp.float32)
    closeness = pair_table[row_cluster[..., :, None], col_cluster[..., None, :]]
    full_shape = (PROW, PCOL, MAXB, BS, BS)
    pick = jax.random.uniform(mask_key, full_shape, jnp.float32)
    level = jax.random.uniform(value_key, full_shape, jnp.float32)
    strong = same & (pick < 0.5)
    slot_factor = jnp.where(jnp.arange(MAXB) >= PROW, 4.0, 1.0).astype(jnp.float32)[None, None, :, None, None]
    floor_level = 0.5 * closeness + 0.5 * level
    floor_value = 0.0001 * jnp.exp(jnp.log(490.0) * floor_level)
    strong_value = jnp.exp(jnp.log(10.0) * (level - 1.0))
    values = jnp.where(strong, strong_value, floor_value)
    values = values * slot_factor
    return values.astype(jnp.float32).astype(jnp.bfloat16)


def draw_labels(key, part):
    cluster = node_clusters(key)
    profile_key, noise_key = jax.random.split(jax.random.fold_in(key, 19))
    profile = jax.random.uniform(profile_key, (cluster_total(), CLASSES), jnp.float32)
    noise = jax.random.uniform(noise_key, (NODES, CLASSES), jnp.float32)
    shared = jnp.take(profile, cluster, axis=0)
    values = 0.5 * noise + 0.5 * shared
    return values.astype(jnp.float32)


def place_ends(values, own_key, smallest, top_value):
    spot = [jax.random.randint(jax.random.fold_in(own_key, axis), (), 0, length) for axis, length in enumerate(values.shape)]
    longest = values.shape.index(max(values.shape))
    next_to = spot[:longest] + [(spot[longest] + 1) % values.shape[longest]] + spot[longest + 1:]
    return values.at[tuple(spot)].set(smallest).at[tuple(next_to)].set(top_value)


def setup_inputs(seed: int = 0) -> dict:
    keys = jax.random.split(jax.random.key(seed), 7)
    return {
        "affinity": draw_affinity(jax.random.fold_in(keys[6], 71), 0),
        "block_rows": draw_block_rows(jax.random.fold_in(keys[6], 71), 0),
        "block_cols": draw_block_cols(jax.random.fold_in(keys[6], 71), 0),
        "block_count": draw_block_count(jax.random.fold_in(keys[6], 71), 0),
        "labels": draw_labels(jax.random.fold_in(keys[6], 71), 0),
        "labelled": place_ends((jax.random.randint(keys[5], (NODES,), 0, 4) < 1).astype(jnp.int32), jax.random.fold_in(keys[5], 1), 0, 1),
    }


spread_weight = 0.8


def placement_table(row_ids, slot_live):
    return ((row_ids[None, :] == jnp.arange(PROW)[:, None]) & slot_live[None, :]).astype(jnp.float32)


def device_term(tile_stack, row_ids, col_ids, live_count, gathered):
    slot_live = jnp.arange(tile_stack.shape[0]) < live_count
    fetched = jnp.take(gathered, col_ids, axis=0).astype(jnp.float32)
    product = jnp.einsum("bij,bjc->bic", tile_stack.astype(jnp.float32), fetched, precision=lax.Precision.HIGHEST)
    placing = placement_table(row_ids, slot_live)
    return jnp.einsum("rb,bic->ric", placing, product, precision=lax.Precision.HIGHEST)


def reference(affinity, block_rows, block_cols, block_count, labels, labelled):
    label_grid = labels.reshape(PROW, PCOL, BS, CLASSES)
    keep_rows = labelled.reshape(PROW, PCOL, BS, 1) == 1

    def add_degree(flat, running):
        grid_row = flat // PCOL
        grid_col = flat % PCOL
        tile_stack = affinity[grid_row, grid_col]
        slot_live = jnp.arange(MAXB) < block_count[grid_row, grid_col]
        row_sums = jnp.sum(tile_stack.astype(jnp.float32), axis=2)
        placing = placement_table(block_rows[grid_row, grid_col], slot_live)
        part_sum = jnp.dot(placing, row_sums, precision=lax.Precision.HIGHEST)
        return running.at[:, grid_col].add(part_sum)

    degree = lax.fori_loop(0, PROW * PCOL, add_degree, jnp.zeros((PROW, PCOL, BS), jnp.float32))
    current = label_grid
    for iteration in range(SWEEPS):
        coarse = current.astype(jnp.bfloat16)

        def add_device(flat, running):
            grid_row = flat // PCOL
            grid_col = flat % PCOL
            gathered = lax.dynamic_index_in_dim(coarse, grid_row, 0, keepdims=False)
            term = device_term(affinity[grid_row, grid_col], block_rows[grid_row, grid_col],
                               block_cols[grid_row, grid_col], block_count[grid_row, grid_col], gathered)
            return running.at[:, grid_col].add(term)

        summed = lax.fori_loop(0, PROW * PCOL, add_device, jnp.zeros((PROW, PCOL, BS, CLASSES), jnp.float32))
        spread = spread_weight * summed / degree[..., None] + (1.0 - spread_weight) * label_grid
        current = jnp.where(keep_rows, label_grid, spread)
    return current.reshape(NODES, CLASSES)
```

```python
import functools

import jax
import jax.numpy as jnp
from jax import lax
from jax.experimental import pallas as pl
from jax.experimental.pallas import tpu as pltpu
from jax.sharding import PartitionSpec as P

SWEEPS = 2
PARTS = [2, 1, 1]
FORWARD = 0
SMALL = 1
ORDER = ("A0", "A1", "D0", "A2", "D1", "U0", "D2", "U1", "D3", "U2", "D4", "D5", "U3", "U4", "U5")
DENSE_LIMIT = 14
TERM_LIMIT = 14
UPDATE_LIMIT = 4
spread_weight = 0.8

COST = None
FREE = pl.CostEstimate(flops=0, bytes_accessed=0, transcendentals=0)
MIB = 1024 * 1024
LANES = 128
PIN = 1


def dense_kernel(slot_ref, tiles_ref, near_tiles_ref, dense_ref, degree_ref, column_ref):
    rows_n = slot_ref.shape[0]
    side = tiles_ref.shape[1]
    places = dense_ref.shape[1] // side
    ones = jnp.ones((8, dense_ref.shape[1]), dense_ref.dtype)
    ones_down = jnp.ones((dense_ref.shape[1], LANES), dense_ref.dtype)

    def line(i, _):
        for e, source in enumerate((tiles_ref, near_tiles_ref)):
            at = pl.ds(pl.multiple_of((e * rows_n + i) * side, side), side)
            for q in range(places):
                slot = slot_ref[i, e * places + q]
                tile = source[jnp.maximum(slot, 0)]
                dense_ref[at, q * side : (q + 1) * side] = jnp.where(slot >= 0, tile, jnp.zeros_like(tile))
            degree_ref[pl.ds(pl.multiple_of((e * rows_n + i) * 8, 8), 8)] = lax.dot_general(
                ones, dense_ref[at], (((1,), (1,)), ((), ())), preferred_element_type=jnp.float32
            )
            column_ref[at] = jnp.dot(dense_ref[at], ones_down, preferred_element_type=jnp.float32)
        return 0

    lax.fori_loop(0, rows_n, line, 0)


def dense_tiles(table, tiles, near_tiles):
    rows_n, places = table.shape
    side = tiles.shape[1]
    dense = jax.ShapeDtypeStruct((2 * rows_n * side, places // 2 * side), tiles.dtype)
    if PIN and dense.size * 2 <= 8 * MIB:
        dense = pltpu.VMEM(dense.shape, dense.dtype)
    return pl.pallas_call(
        dense_kernel,
        out_shape=[
            dense,
            jax.ShapeDtypeStruct((2 * rows_n * 8, side), jnp.float32),
            jax.ShapeDtypeStruct((2 * rows_n * side, LANES), jnp.float32),
        ],
        in_specs=[pl.BlockSpec(memory_space=pltpu.SMEM)] + [pl.BlockSpec(memory_space=pltpu.VMEM)] * 2,
        out_specs=[pl.BlockSpec(memory_space=pltpu.VMEM)] * 3,
        compiler_params=pltpu.CompilerParams(vmem_limit_bytes=(DENSE_LIMIT if dense.shape[0] * dense.shape[1] <= 4 * MIB else 56) * MIB),
        cost_estimate=FREE,
    )(table, tiles, near_tiles)


def term_kernel(count, rows_n, extra, token_ref, dense_ref, *refs):
    block_refs, extra_refs = refs[:count], refs[count : count + extra]
    next_ref, *term_refs = refs[count + extra :]
    next_ref[...] = token_ref[...]
    blocks = [r[...] for r in block_refs]
    if count == 5:
        blocks = blocks[:3] + [blocks[3] + blocks[4]]
    depth = blocks[0].shape[0]
    side = depth // 2
    for e in range(2):
        lines = slice(e * rows_n * side, (e + 1) * rows_n * side)
        total = None
        for k, block in enumerate(blocks):
            product = jnp.dot(
                dense_ref[lines, k * depth : (k + 1) * depth], block, preferred_element_type=jnp.float32
            )
            total = product if total is None else total + product
        for m, term_ref in enumerate(term_refs):
            term_ref[e * side : (e + 1) * side] = total[m * side : (m + 1) * side]
    for extra_ref, term_ref in zip(extra_refs, term_refs):
        term_ref[depth:] = extra_ref[...]


def term_step_kernel(count, rows_n, extra, token_ref, dense_ref, *refs):
    block_refs, extra_refs = refs[:count], refs[count : count + extra]
    next_ref, *term_refs = refs[count + extra :]
    next_ref[...] = token_ref[...]
    depth = block_refs[0].shape[0]
    side = depth // 2
    e, line = pl.program_id(0), pl.program_id(1)
    total = None
    for k, block_ref in enumerate(block_refs):
        product = jnp.dot(
            dense_ref[:, k * depth : (k + 1) * depth], block_ref[...], preferred_element_type=jnp.float32
        )
        total = product if total is None else total + product
    for m, term_ref in enumerate(term_refs):

        @pl.when(line == m)
        def _():
            term_ref[pl.ds(pl.multiple_of(e * side, side), side)] = total
            if extra:
                term_ref[depth:] = extra_refs[m][...]


def terms(token, dense, blocks, extras, rows_n):
    side = dense.shape[0] // (2 * rows_n)
    width = blocks[0].shape[1]
    rows = 2 * side + (extras[0].shape[0] if extras else 0)
    whole = dense.size * 2 <= 8 * MIB
    vmem = pl.BlockSpec(memory_space=pltpu.VMEM)
    others = len(blocks) + len(extras)
    if whole:
        dense = pltpu.with_memory_space_constraint(dense, pltpu.VMEM) if PIN else dense
        split = dict(in_specs=[vmem] * (2 + others), out_specs=[vmem] * (1 + rows_n))
    else:
        at_start = lambda x: pl.BlockSpec(x.shape, lambda e, m: (0, 0))
        out = jax.ShapeDtypeStruct((rows, width), jnp.float32)
        split = dict(
            grid=(2, rows_n),
            in_specs=[at_start(token), pl.BlockSpec((side, dense.shape[1]), lambda e, m: (e * rows_n + m, 0))]
            + [at_start(x) for x in (*blocks, *extras)],
            out_specs=[at_start(token)] + [at_start(out)] * rows_n,
        )
    token, *out = pl.pallas_call(
        functools.partial(term_kernel if whole else term_step_kernel, len(blocks), rows_n, len(extras)),
        out_shape=[jax.ShapeDtypeStruct(token.shape, token.dtype)]
        + [jax.ShapeDtypeStruct((rows, width), jnp.float32)] * rows_n,
        compiler_params=pltpu.CompilerParams(vmem_limit_bytes=(TERM_LIMIT if whole else 48) * MIB),
        cost_estimate=None if COST is None else pl.CostEstimate(flops=int(COST * 1e9 * width / 512), bytes_accessed=0, transcendentals=0),
        **split,
    )(token, dense, *blocks, *extras)
    return token, out


def begin_kernel(token_ref, kept_ref, got_ref, next_ref, prior_ref, coarse_ref):
    side = kept_ref.shape[0]
    next_ref[...] = token_ref[...]
    for k, ref in enumerate((kept_ref, got_ref)):
        prior_ref[k * side : (k + 1) * side] = ref[...]
        coarse_ref[k * side : (k + 1) * side] = ref[...].astype(jnp.bfloat16)


def begin(token, kept, got):
    rows, width = 2 * kept.shape[0], kept.shape[1]
    vmem = pl.BlockSpec(memory_space=pltpu.VMEM)
    return pl.pallas_call(
        begin_kernel,
        out_shape=[
            jax.ShapeDtypeStruct(token.shape, token.dtype),
            jax.ShapeDtypeStruct((rows, width), jnp.float32),
            jax.ShapeDtypeStruct((rows, width), jnp.bfloat16),
        ],
        in_specs=[vmem] * 3,
        out_specs=[vmem] * 3,
        compiler_params=pltpu.CompilerParams(vmem_limit_bytes=UPDATE_LIMIT * MIB),
        cost_estimate=FREE,
    )(token, kept, got)


def update_kernel(token_ref, keep_ref, scale_ref, prior_ref, own_ref, *refs):
    *got_refs, next_ref, out_ref = refs
    next_ref[...] = token_ref[...]
    spread(keep_ref, scale_ref, prior_ref, own_ref, got_refs, out_ref)


def spread(keep_ref, scale_ref, prior_ref, own_ref, got_refs, out_ref):
    rows, width = out_ref.shape
    for at in range(0, width, LANES):
        lanes = slice(at, at + LANES)
        summed = own_ref[:rows, lanes]
        for got_ref in got_refs:
            summed += got_ref[:rows, lanes]
        prior = prior_ref[:, lanes]
        value = scale_ref[...] * summed + (1.0 - spread_weight) * prior
        out_ref[:, lanes] = jnp.where(keep_ref[...] > 0, prior, value).astype(out_ref.dtype)


def first_update_kernel(count, token_ref, labelled_ref, prior_ref, *refs):
    term_refs, (next_ref, out_ref, keep_ref, scale_ref, *column_refs) = refs[:count], refs[count:]
    next_ref[...] = token_ref[...]
    rows, width = out_ref.shape

    def turn(ref, first):
        for at in range(0, rows, LANES):
            line, lane = first + at // ref.shape[1], at % ref.shape[1]
            flat = jnp.broadcast_to(ref[line : line + 1, lane : lane + LANES], (LANES, LANES))
            yield slice(at, at + LANES), flat.T

    for at, column in turn(labelled_ref, 0):
        keep_ref[at] = column
    for term_ref, column_ref in zip(term_refs, column_refs):
        for at, column in turn(term_ref, rows):
            column_ref[at] = column
    total = column_refs[0][...]
    for column_ref in column_refs[1:]:
        total += column_ref[...]
    scale_ref[...] = spread_weight / total
    spread(keep_ref, scale_ref, prior_ref, term_refs[0], term_refs[1:], out_ref)


def update(token, keep, scale, prior, own, got):
    vmem = pl.BlockSpec(memory_space=pltpu.VMEM)
    return pl.pallas_call(
        update_kernel,
        out_shape=[
            jax.ShapeDtypeStruct(token.shape, token.dtype),
            jax.ShapeDtypeStruct(prior.shape, jnp.bfloat16),
        ],
        in_specs=[vmem] * (5 + len(got)),
        out_specs=[vmem] * 2,
        compiler_params=pltpu.CompilerParams(vmem_limit_bytes=UPDATE_LIMIT * MIB),
        cost_estimate=FREE,
    )(token, keep, scale, prior, own, *got)


def first_update(token, labelled, prior, terms_in):
    vmem = pl.BlockSpec(memory_space=pltpu.VMEM)
    column = jax.ShapeDtypeStruct((prior.shape[0], LANES), jnp.float32)
    return pl.pallas_call(
        functools.partial(first_update_kernel, len(terms_in)),
        out_shape=[
            jax.ShapeDtypeStruct(token.shape, token.dtype),
            jax.ShapeDtypeStruct(prior.shape, jnp.bfloat16),
        ]
        + [column] * (2 + len(terms_in)),
        in_specs=[vmem] * (3 + len(terms_in)),
        out_specs=[vmem] * (4 + len(terms_in)),
        compiler_params=pltpu.CompilerParams(vmem_limit_bytes=2 * UPDATE_LIMIT * MIB),
        cost_estimate=FREE,
    )(token, labelled, prior, *terms_in)


def swap(x, axis, mask):
    size = lax.axis_size(axis)
    return lax.ppermute(x, axis, [(i, i ^ mask) for i in range(size)])


def on_device(affinity, block_rows, block_cols, block_count, labels, labelled):
    tiles = affinity[0, 0]
    rows_n = lax.axis_size("row")
    cols_n = lax.axis_size("col")
    slots, side, _ = tiles.shape
    half = labels.shape[1] // 2
    row, col = lax.axis_index("row"), lax.axis_index("col")
    core = col & 1

    count = len(PARTS)
    widths = [half * p // sum(PARTS) for p in PARTS]
    starts = [sum(widths[:i]) for i in range(count)]
    halves = []
    for s, w in zip(starts, widths):
        kept = lax.dynamic_slice_in_dim(labels, core * half + s, w, 1)
        given = lax.dynamic_slice_in_dim(labels, (1 - core) * half + s, w, 1)
        halves.append((kept, swap(given, "col", 1)))

    live = jnp.arange(slots) < block_count[0, 0]
    hit = (
        ((block_rows[0, 0] ^ row)[None, None, :] == jnp.arange(rows_n)[:, None, None])
        & ((block_cols[0, 0] ^ col)[None, None, :] == jnp.arange(cols_n)[None, :, None])
        & live[None, None, :]
    )
    table = jnp.max(jnp.where(hit, jnp.arange(slots), -1), axis=2).astype(jnp.int32)
    near_tiles = swap(tiles, "col", 1)
    numbers = jnp.concatenate([table.reshape(-1), labelled])
    near_numbers = swap(numbers, "col", 1)
    near_table = near_numbers[: rows_n * cols_n].reshape(rows_n, cols_n // 2, 2)
    near_table = near_table[:, :, ::-1].reshape(rows_n, cols_n)
    table = jnp.concatenate([table, near_table], axis=1)
    both = jnp.concatenate([labelled, near_numbers[rows_n * cols_n :]])
    both = jnp.pad((both == 1).astype(jnp.float32).reshape(-1, LANES), ((0, -(2 * side // LANES) % 8), (0, 0)))
    inner = [i for i in range(cols_n) if (i >> 1) & 3 in (1, 2)]

    dense, part, columns = dense_tiles(table, tiles, near_tiles)
    part = part.reshape(2, rows_n, 8, side)[:, :, 0]
    part = [part[:, m].reshape(2 * side) for m in range(rows_n)]
    columns = columns.reshape(2, rows_n, side, LANES)
    columns = [columns[:, m].reshape(2 * side, LANES) for m in range(rows_n)]

    def wide(x, width):
        return jnp.concatenate([x] * (width // LANES), axis=1)

    token = start = jnp.zeros((8, 128), jnp.float32)
    priors, held, sums, final = {}, {}, {}, {}
    degrees = None

    def spread_out(x):
        if FORWARD:
            far = swap(x, "col", 4)
            blocks = [
                x,
                swap(x, "col", 2),
                far,
                lax.ppermute(x, "col", [(i, i ^ 6) for i in inner]),
                lax.ppermute(far, "col", [(i, i ^ 2) for i in inner]),
            ]
            if cols_n > 8:
                blocks = blocks[:3] + [blocks[3] + blocks[4]]
        else:
            blocks = [x] + [swap(x, "col", 2 * k) for k in range(1, min(4, cols_n // 2))]
        while 4 <= len(blocks) < cols_n // 2:
            blocks = blocks + [swap(b, "col", 2 * len(blocks)) for b in blocks]
        return blocks

    for name in ORDER:
        kind, n = name[0], int(name[1:])
        c, last = n % count, n >= count * (SWEEPS - 1)
        width = widths[c]
        free, token = token, (start if kind.islower() else token)
        kind = kind.upper()
        if kind == "A":
            token, priors[c], coarse = begin(token, *halves[c])
            held[n] = spread_out(coarse)
        elif kind == "D":
            extras = []
            if degrees is None:
                lines = 2 * side // width
                extras = [jnp.pad(p.reshape(lines, width), ((0, -lines % 8), (0, 0))) for p in part]
                degrees = n
            token, term = terms(token, dense, held.pop(n), extras, rows_n)
            if last and SMALL:
                sent = [(t / wide(p, width)).astype(jnp.float16) for t, p in zip(term[1:], columns[1:])]
            else:
                sent = term[1:]
            sums[n] = [term[0]] + [swap(x, "row", m + 1) for m, x in enumerate(sent)]
        elif not last:
            if n == degrees:
                token, coarse, keep, scale, *degrees = first_update(token, both, priors[c], sums.pop(n))
            else:
                own, *got = sums.pop(n)
                token, coarse = update(token, keep, scale, priors[c], own, got)
            held[n + count] = spread_out(coarse)
        else:
            own, *got = sums.pop(n)
            if SMALL:
                got = [x.astype(jnp.float32) * wide(p, width) for x, p in zip(got, degrees[1:])]
            prior = priors[c]
            out = jnp.where(
                wide(keep, width) > 0,
                prior,
                wide(scale, width) * (own + sum(got)) + (1.0 - spread_weight) * prior,
            )
            final[c] = out[:side], swap(out[side:], "col", 1)
        if name[0].islower():
            token = free
    final = [final[c] for c in range(count)]
    mine, other = (jnp.concatenate([f[k] for f in final], axis=1) for k in (0, 1))
    low, high = jnp.where(core == 0, mine, other), jnp.where(core == 0, other, mine)
    return jnp.concatenate([low, high], axis=1)


def solution(mesh):
    placed = (
        P("row", "col", None, None, None),
        P("row", "col", None),
        P("row", "col", None),
        P("row", "col"),
        P(("row", "col"), None),
        P(("row", "col")),
    )
    return jax.shard_map(
        on_device, mesh=mesh, in_specs=placed, out_specs=P(("row", "col"), None), check_vma=False
    )
```

```python
import functools
import math

import jax
import jax.numpy as jnp
from jax import lax
from jax.experimental import pallas as pl
from jax.experimental.pallas import tpu as pltpu
from jax.sharding import PartitionSpec as P

SWEEPS = 2
PARTS = [1, 1]
FORWARD = 0
ORDER = ("A0", "A1", "G", "D0", "U0", "D1", "D2", "U1", "D3", "U2", "U3")
DENSE_LIMIT = 14
TERM_LIMIT = 14
UPDATE_LIMIT = 4
spread_weight = 0.8

COST = None
FREE = pl.CostEstimate(flops=0, bytes_accessed=0, transcendentals=0)
MIB = 1024 * 1024
LANES = 128
STEP = 235.0
SHIFT = 2.0**-62.5
PIN = 0
PIN_IN = 0


def dense_kernel(slot_ref, tiles_ref, near_tiles_ref, dense_ref, column_ref, *degree_refs):
    rows_n = slot_ref.shape[0]
    side = tiles_ref.shape[1]
    places = dense_ref.shape[1] // side
    ones = jnp.ones((8, dense_ref.shape[1]), dense_ref.dtype)
    ones_down = jnp.ones((dense_ref.shape[1], LANES), dense_ref.dtype)

    def line(i, _):
        for e, source in enumerate((tiles_ref, near_tiles_ref)):
            at = pl.ds(pl.multiple_of((e * rows_n + i) * side, side), side)
            for q in range(places):
                slot = slot_ref[i, e * places + q]
                tile = source[jnp.maximum(slot, 0)]
                dense_ref[at, q * side : (q + 1) * side] = jnp.where(slot >= 0, tile, jnp.zeros_like(tile))
            degree = lax.dot_general(
                ones, dense_ref[at], (((1,), (1,)), ((), ())), preferred_element_type=jnp.float32
            )
            for m, degree_ref in enumerate(degree_refs):

                @pl.when(i == m)
                def _():
                    for k in range(side // LANES):
                        to = e * (side // LANES) + k
                        degree_ref[to : to + 1] = degree[:1, k * LANES : (k + 1) * LANES]

            column_ref[at] = 1.0 / jnp.dot(dense_ref[at], ones_down, preferred_element_type=jnp.float32)
        return 0

    lax.fori_loop(0, rows_n, line, 0)


def dense_tiles(table, tiles, near_tiles):
    rows_n, places = table.shape
    side = tiles.shape[1]
    dense = jax.ShapeDtypeStruct((2 * rows_n * side, places // 2 * side), tiles.dtype)
    if PIN and dense.size * 2 <= 8 * MIB:
        dense = pltpu.VMEM(dense.shape, dense.dtype)
    return pl.pallas_call(
        dense_kernel,
        out_shape=[
            dense,
            jax.ShapeDtypeStruct((2 * rows_n * side, LANES), jnp.float32),
        ]
        + [jax.ShapeDtypeStruct((-(-2 * side // LANES // 8) * 8, LANES), jnp.float32)] * rows_n,
        in_specs=[pl.BlockSpec(memory_space=pltpu.SMEM)] + [pl.BlockSpec(memory_space=pltpu.VMEM)] * 2,
        out_specs=[pl.BlockSpec(memory_space=pltpu.VMEM)] * (2 + rows_n),
        compiler_params=pltpu.CompilerParams(vmem_limit_bytes=(DENSE_LIMIT if dense.shape[0] * dense.shape[1] <= 4 * MIB else 56) * MIB),
        cost_estimate=FREE,
    )(table, tiles, near_tiles)


def encode(value, inverse, code_ref, rows, scale_rows):
    lanes = [slice(at, at + LANES) for at in range(0, value.shape[1], LANES)]
    parts = [value[:, at] * inverse for at in lanes]
    top = jnp.max(functools.reduce(jnp.maximum, parts), axis=(0, 1), keepdims=True)
    top = jnp.broadcast_to(jnp.maximum(top, 1e-30), (16, LANES)).astype(jnp.bfloat16)
    factor = STEP / top.astype(jnp.float32)[:1]
    for at, part in zip(lanes, parts):
        power = 1.0 + part * factor
        for _ in range(4):
            power = power * power
        power = power * SHIFT
        code_ref[rows, at] = (power * power).astype(jnp.bfloat16)
        code_ref[scale_rows, at] = top


def decode(code_ref, rows, scale_row, at):
    top = code_ref[scale_row : scale_row + 16, at].astype(jnp.float32)[:1]
    power = jnp.log(code_ref[rows, at].astype(jnp.float32)) - 2.0 * math.log(SHIFT)
    return (jnp.exp(power * (1.0 / 32.0)) - 1.0) * (top * (1.0 / STEP))


def term_kernel(count, rows_n, token_ref, dense_ref, inverse_ref, *refs):
    block_refs, (next_ref, own_ref, *code_refs) = refs[:count], refs[count:]
    next_ref[...] = token_ref[...]
    blocks = [r[...] for r in block_refs]
    if count == 5:
        blocks = blocks[:3] + [blocks[3] + blocks[4]]
    depth = blocks[0].shape[0]
    side = depth // 2
    for e in range(2):
        lines = slice(e * rows_n * side, (e + 1) * rows_n * side)
        total = None
        for k, block in enumerate(blocks):
            product = jnp.dot(
                dense_ref[lines, k * depth : (k + 1) * depth], block, preferred_element_type=jnp.float32
            )
            total = product if total is None else total + product
        rows = slice(e * side, (e + 1) * side)
        own_ref[rows] = total[:side]
        for m, code_ref in enumerate(code_refs, 1):
            line = slice((e * rows_n + m) * side, (e * rows_n + m + 1) * side)
            scale_rows = slice(depth + 16 * e, depth + 16 * (e + 1))
            encode(total[m * side : (m + 1) * side], inverse_ref[line], code_ref, rows, scale_rows)


def term_step_kernel(count, rows_n, token_ref, dense_ref, inverse_ref, *refs):
    block_refs, (next_ref, own_ref, *code_refs) = refs[:count], refs[count:]
    next_ref[...] = token_ref[...]
    depth = block_refs[0].shape[0]
    side = depth // 2
    e, line = pl.program_id(0), pl.program_id(1)
    total = None
    for k, block_ref in enumerate(block_refs):
        product = jnp.dot(
            dense_ref[:, k * depth : (k + 1) * depth], block_ref[...], preferred_element_type=jnp.float32
        )
        total = product if total is None else total + product
    rows = pl.ds(pl.multiple_of(e * side, side), side)
    scale_rows = pl.ds(pl.multiple_of(depth + 16 * e, 16), 16)

    @pl.when(line == 0)
    def _():
        own_ref[rows] = total

    for m, code_ref in enumerate(code_refs, 1):

        @pl.when(line == m)
        def _():
            encode(total, inverse_ref[...], code_ref, rows, scale_rows)


def terms(token, dense, inverse, blocks, rows_n):
    side = dense.shape[0] // (2 * rows_n)
    width = blocks[0].shape[1]
    whole = dense.size * 2 <= 8 * MIB
    vmem = pl.BlockSpec(memory_space=pltpu.VMEM)
    own = jax.ShapeDtypeStruct((2 * side, width), jnp.float32)
    code = jax.ShapeDtypeStruct((2 * side + 32, width), jnp.bfloat16)
    if whole and PIN_IN:
        dense = pltpu.with_memory_space_constraint(dense, pltpu.VMEM)
    if whole:
        split = dict(in_specs=[vmem] * (3 + len(blocks)), out_specs=[vmem] * (1 + rows_n))
    else:
        at_start = lambda x: pl.BlockSpec(x.shape, lambda e, m: (0, 0))
        split = dict(
            grid=(2, rows_n),
            in_specs=[
                at_start(token),
                pl.BlockSpec((side, dense.shape[1]), lambda e, m: (e * rows_n + m, 0)),
                pl.BlockSpec((side, LANES), lambda e, m: (e * rows_n + m, 0)),
            ]
            + [at_start(x) for x in blocks],
            out_specs=[at_start(token), at_start(own)] + [at_start(code)] * (rows_n - 1),
        )
    token, *out = pl.pallas_call(
        functools.partial(term_kernel if whole else term_step_kernel, len(blocks), rows_n),
        out_shape=[jax.ShapeDtypeStruct(token.shape, token.dtype), own] + [code] * (rows_n - 1),
        compiler_params=pltpu.CompilerParams(vmem_limit_bytes=(TERM_LIMIT if whole else 48) * MIB),
        cost_estimate=FREE,
        **split,
    )(token, dense, inverse, *blocks)
    return token, out


def after(token, waited):
    anywhere = pl.BlockSpec(memory_space=pl.ANY)
    vmem = pl.BlockSpec(memory_space=pltpu.VMEM)

    def kernel(token_ref, waited_ref, next_ref):
        next_ref[...] = token_ref[...]

    return pl.pallas_call(
        kernel,
        out_shape=jax.ShapeDtypeStruct(token.shape, token.dtype),
        in_specs=[vmem, anywhere],
        out_specs=vmem,
        compiler_params=pltpu.CompilerParams(vmem_limit_bytes=MIB),
        cost_estimate=FREE,
    )(token, waited)


def begin_kernel(token_ref, kept_ref, got_ref, next_ref, prior_ref, coarse_ref):
    side = kept_ref.shape[0]
    next_ref[...] = token_ref[...]
    for k, ref in enumerate((kept_ref, got_ref)):
        prior_ref[k * side : (k + 1) * side] = ref[...]
        coarse_ref[k * side : (k + 1) * side] = ref[...].astype(jnp.bfloat16)


def begin(token, kept, got):
    rows, width = 2 * kept.shape[0], kept.shape[1]
    vmem = pl.BlockSpec(memory_space=pltpu.VMEM)
    return pl.pallas_call(
        begin_kernel,
        out_shape=[
            jax.ShapeDtypeStruct(token.shape, token.dtype),
            jax.ShapeDtypeStruct((rows, width), jnp.float32),
            jax.ShapeDtypeStruct((rows, width), jnp.bfloat16),
        ],
        in_specs=[vmem] * 3,
        out_specs=[vmem] * 3,
        compiler_params=pltpu.CompilerParams(vmem_limit_bytes=UPDATE_LIMIT * MIB),
        cost_estimate=FREE,
    )(token, kept, got)


def update_kernel(count, token_ref, keep_ref, scale_ref, prior_ref, own_ref, *refs):
    code_refs, degree_refs, (next_ref, out_ref) = refs[:count], refs[count : 2 * count], refs[2 * count :]
    next_ref[...] = token_ref[...]
    depth, width = out_ref.shape
    side = depth // 2
    for e in range(2):
        rows = slice(e * side, (e + 1) * side)
        for at in range(0, width, LANES):
            lanes = slice(at, at + LANES)
            summed = own_ref[rows, lanes]
            for code_ref, degree_ref in zip(code_refs, degree_refs):
                summed += decode(code_ref, rows, depth + 16 * e, lanes) * degree_ref[rows]
            prior = prior_ref[rows, lanes]
            value = scale_ref[rows] * summed + (1.0 - spread_weight) * prior
            out_ref[rows, lanes] = jnp.where(keep_ref[rows] > 0, prior, value).astype(out_ref.dtype)


def update(token, keep, scale, prior, own, codes, degrees, dtype):
    vmem = pl.BlockSpec(memory_space=pltpu.VMEM)
    return pl.pallas_call(
        functools.partial(update_kernel, len(codes)),
        out_shape=[
            jax.ShapeDtypeStruct(token.shape, token.dtype),
            jax.ShapeDtypeStruct(prior.shape, dtype),
        ],
        in_specs=[vmem] * (5 + 2 * len(codes)),
        out_specs=[vmem] * 2,
        compiler_params=pltpu.CompilerParams(vmem_limit_bytes=2 * UPDATE_LIMIT * MIB),
        cost_estimate=FREE,
    )(token, keep, scale, prior, own, *codes, *degrees)


def columns_kernel(token_ref, labelled_ref, *refs):
    row_refs, (next_ref, keep_ref, scale_ref, *column_refs) = refs[: len(refs) // 2 - 1], refs[len(refs) // 2 - 1 :]
    next_ref[...] = token_ref[...]

    def turn(ref, out_ref):
        for k in range(out_ref.shape[0] // LANES):
            flat = jnp.broadcast_to(ref[k : k + 1], (LANES, LANES))
            out_ref[k * LANES : (k + 1) * LANES] = flat.T

    turn(labelled_ref, keep_ref)
    turn(row_refs[0], scale_ref)
    total = scale_ref[...]
    for row_ref, column_ref in zip(row_refs[1:], column_refs):
        turn(row_ref, column_ref)
        total += column_ref[...]
    scale_ref[...] = spread_weight / total


def columns(token, labelled, rows, depth):
    vmem = pl.BlockSpec(memory_space=pltpu.VMEM)
    return pl.pallas_call(
        columns_kernel,
        out_shape=[jax.ShapeDtypeStruct(token.shape, token.dtype)]
        + [jax.ShapeDtypeStruct((depth, LANES), jnp.float32)] * (1 + len(rows)),
        in_specs=[vmem] * (2 + len(rows)),
        out_specs=[vmem] * (2 + len(rows)),
        compiler_params=pltpu.CompilerParams(vmem_limit_bytes=UPDATE_LIMIT * MIB),
        cost_estimate=FREE,
    )(token, labelled, *rows)


def swap(x, axis, mask):
    size = lax.axis_size(axis)
    return lax.ppermute(x, axis, [(i, i ^ mask) for i in range(size)])


def on_device(affinity, block_rows, block_cols, block_count, labels, labelled):
    tiles = affinity[0, 0]
    rows_n = lax.axis_size("row")
    cols_n = lax.axis_size("col")
    slots, side, _ = tiles.shape
    half = labels.shape[1] // 2
    row, col = lax.axis_index("row"), lax.axis_index("col")
    core = col & 1

    count = len(PARTS)
    widths = [half * p // sum(PARTS) for p in PARTS]
    starts = [sum(widths[:i]) for i in range(count)]
    halves = []
    for s, w in zip(starts, widths):
        kept = lax.dynamic_slice_in_dim(labels, core * half + s, w, 1)
        given = lax.dynamic_slice_in_dim(labels, (1 - core) * half + s, w, 1)
        halves.append((kept, swap(given, "col", 1)))

    live = jnp.arange(slots) < block_count[0, 0]
    hit = (
        ((block_rows[0, 0] ^ row)[None, None, :] == jnp.arange(rows_n)[:, None, None])
        & ((block_cols[0, 0] ^ col)[None, None, :] == jnp.arange(cols_n)[None, :, None])
        & live[None, None, :]
    )
    table = jnp.max(jnp.where(hit, jnp.arange(slots), -1), axis=2).astype(jnp.int32)
    near_tiles = swap(tiles, "col", 1)
    numbers = jnp.concatenate([table.reshape(-1), labelled])
    near_numbers = swap(numbers, "col", 1)
    near_table = near_numbers[: rows_n * cols_n].reshape(rows_n, cols_n // 2, 2)
    near_table = near_table[:, :, ::-1].reshape(rows_n, cols_n)
    table = jnp.concatenate([table, near_table], axis=1)
    both = jnp.concatenate([labelled, near_numbers[rows_n * cols_n :]])
    both = jnp.pad((both == 1).astype(jnp.float32).reshape(-1, LANES), ((0, -(2 * side // LANES) % 8), (0, 0)))
    inner = [i for i in range(cols_n) if (i >> 1) & 3 in (1, 2)]

    dense, inverse, *part = dense_tiles(table, tiles, near_tiles)
    part = [part[0]] + [swap(part[m], "row", m) for m in range(1, rows_n)]
    token = start = jnp.zeros((8, 128), jnp.float32)
    priors, held, sums, final = {}, {}, {}, {}

    def spread_out(x):
        if FORWARD:
            far = swap(x, "col", 4)
            blocks = [
                x,
                swap(x, "col", 2),
                far,
                lax.ppermute(x, "col", [(i, i ^ 6) for i in inner]),
                lax.ppermute(far, "col", [(i, i ^ 2) for i in inner]),
            ]
            if cols_n > 8:
                blocks = blocks[:3] + [blocks[3] + blocks[4]]
        else:
            blocks = [x] + [swap(x, "col", 2 * k) for k in range(1, min(4, cols_n // 2))]
        while 4 <= len(blocks) < cols_n // 2:
            blocks = blocks + [swap(b, "col", 2 * len(blocks)) for b in blocks]
        return blocks

    for name in ORDER:
        if name == "G":
            token, keep, scale, *degrees = columns(token, both, part, 2 * side)
            continue
        kind, n = name[0], int(name[1:].split(".")[0])
        c, last = n % count, n >= count * (SWEEPS - 1)
        free, token = token, (start if kind.islower() else token)
        kind = kind.upper()
        if kind == "W":
            token = after(token, held[n][int(name.split(".")[1])])
        elif kind == "A":
            token, priors[c], coarse = begin(token, *halves[c])
            held[n] = spread_out(coarse)
        elif kind == "D":
            token, (own, *codes) = terms(token, dense, inverse, held.pop(n), rows_n)
            sums[n] = own, [swap(x, "row", m) for m, x in enumerate(codes, 1)]
        else:
            dtype = jnp.float32 if last else jnp.bfloat16
            token, out = update(token, keep, scale, priors[c], *sums.pop(n), degrees, dtype)
            if last:
                final[c] = out[:side], swap(out[side:], "col", 1)
            else:
                held[n + count] = spread_out(out)
        if name[0].islower():
            token = free
    final = [final[c] for c in range(count)]
    mine, other = (jnp.concatenate([f[k] for f in final], axis=1) for k in (0, 1))
    low, high = jnp.where(core == 0, mine, other), jnp.where(core == 0, other, mine)
    return jnp.concatenate([low, high], axis=1)


def solution(mesh):
    placed = (
        P("row", "col", None, None, None),
        P("row", "col", None),
        P("row", "col", None),
        P("row", "col"),
        P(("row", "col"), None),
        P(("row", "col")),
    )
    return jax.shard_map(
        on_device, mesh=mesh, in_specs=placed, out_specs=P(("row", "col"), None), check_vma=False
    )
```

```python
import functools
import math

import jax
import jax.numpy as jnp
from jax import lax
from jax.experimental import pallas as pl
from jax.experimental.pallas import tpu as pltpu
from jax.sharding import PartitionSpec as P

SWEEPS = 2
PARTS = [1, 1]
FORWARD = 0
ORDER = ("A0", "A1", "G", "D0", "U0", "D1", "D2", "U1", "D3", "U2", "U3")
DENSE_LIMIT = 14
TERM_LIMIT = 14
UPDATE_LIMIT = 4
spread_weight = 0.8

COST = None
FREE = pl.CostEstimate(flops=0, bytes_accessed=0, transcendentals=0)
MIB = 1024 * 1024
LANES = 128
STEP = 235.0
SHIFT = 2.0**-62.5
PIN = 0
PIN_IN = 0


def dense_kernel(slot_ref, tiles_ref, near_tiles_ref, dense_ref, column_ref, *degree_refs):
    rows_n = slot_ref.shape[0]
    side = tiles_ref.shape[1]
    places = dense_ref.shape[1] // side
    ones = jnp.ones((8, dense_ref.shape[1]), dense_ref.dtype)
    ones_down = jnp.ones((dense_ref.shape[1], LANES), dense_ref.dtype)

    def line(i, _):
        for e, source in enumerate((tiles_ref, near_tiles_ref)):
            at = pl.ds(pl.multiple_of((e * rows_n + i) * side, side), side)
            for q in range(places):
                slot = slot_ref[i, e * places + q]
                tile = source[jnp.maximum(slot, 0)]
                dense_ref[at, q * side : (q + 1) * side] = jnp.where(slot >= 0, tile, jnp.zeros_like(tile))
            degree = lax.dot_general(
                ones, dense_ref[at], (((1,), (1,)), ((), ())), preferred_element_type=jnp.float32
            )
            for m, degree_ref in enumerate(degree_refs):

                @pl.when(i == m)
                def _():
                    for k in range(side // LANES):
                        to = e * (side // LANES) + k
                        degree_ref[to : to + 1] = degree[:1, k * LANES : (k + 1) * LANES]

            column_ref[at] = 1.0 / jnp.dot(dense_ref[at], ones_down, preferred_element_type=jnp.float32)
        return 0

    lax.fori_loop(0, rows_n, line, 0)


def dense_tiles(table, tiles, near_tiles):
    rows_n, places = table.shape
    side = tiles.shape[1]
    dense = jax.ShapeDtypeStruct((2 * rows_n * side, places // 2 * side), tiles.dtype)
    if PIN and dense.size * 2 <= 8 * MIB:
        dense = pltpu.VMEM(dense.shape, dense.dtype)
    return pl.pallas_call(
        dense_kernel,
        out_shape=[
            dense,
            jax.ShapeDtypeStruct((2 * rows_n * side, LANES), jnp.float32),
        ]
        + [jax.ShapeDtypeStruct((-(-2 * side // LANES // 8) * 8, LANES), jnp.float32)] * rows_n,
        in_specs=[pl.BlockSpec(memory_space=pltpu.SMEM)] + [pl.BlockSpec(memory_space=pltpu.VMEM)] * 2,
        out_specs=[pl.BlockSpec(memory_space=pltpu.VMEM)] * (2 + rows_n),
        compiler_params=pltpu.CompilerParams(vmem_limit_bytes=(DENSE_LIMIT if dense.shape[0] * dense.shape[1] <= 4 * MIB else 56) * MIB),
        cost_estimate=FREE,
    )(table, tiles, near_tiles)


def encode(value, inverse, code_ref, rows, scale_rows):
    lanes = [slice(at, at + LANES) for at in range(0, value.shape[1], LANES)]
    parts = [value[:, at] * inverse for at in lanes]
    top = jnp.max(functools.reduce(jnp.maximum, parts), axis=(0, 1), keepdims=True)
    top = jnp.broadcast_to(jnp.maximum(top, 1e-30), (16, LANES)).astype(jnp.bfloat16)
    factor = STEP / top.astype(jnp.float32)[:1]
    for at, part in zip(lanes, parts):
        power = 1.0 + part * factor
        for _ in range(4):
            power = power * power
        power = power * SHIFT
        code_ref[rows, at] = (power * power).astype(jnp.bfloat16)
        code_ref[scale_rows, at] = top


def decode(code_ref, rows, scale_row, at):
    top = code_ref[scale_row : scale_row + 16, at].astype(jnp.float32)[:1]
    power = jnp.log(code_ref[rows, at].astype(jnp.float32)) - 2.0 * math.log(SHIFT)
    return (jnp.exp(power * (1.0 / 32.0)) - 1.0) * (top * (1.0 / STEP))


def term_kernel(count, rows_n, token_ref, dense_ref, inverse_ref, *refs):
    block_refs, (next_ref, own_ref, *code_refs) = refs[:count], refs[count:]
    next_ref[...] = token_ref[...]
    blocks = [r[...] for r in block_refs]
    if count == 5:
        blocks = blocks[:3] + [blocks[3] + blocks[4]]
    depth = blocks[0].shape[0]
    side = depth // 2
    for e in range(2):
        lines = slice(e * rows_n * side, (e + 1) * rows_n * side)
        total = None
        for k, block in enumerate(blocks):
            product = jnp.dot(
                dense_ref[lines, k * depth : (k + 1) * depth], block, preferred_element_type=jnp.float32
            )
            total = product if total is None else total + product
        rows = slice(e * side, (e + 1) * side)
        own_ref[rows] = total[:side]
        for m, code_ref in enumerate(code_refs, 1):
            line = slice((e * rows_n + m) * side, (e * rows_n + m + 1) * side)
            scale_rows = slice(depth + 16 * e, depth + 16 * (e + 1))
            encode(total[m * side : (m + 1) * side], inverse_ref[line], code_ref, rows, scale_rows)


def term_step_kernel(count, rows_n, token_ref, dense_ref, inverse_ref, *refs):
    block_refs, (next_ref, own_ref, *code_refs) = refs[:count], refs[count:]
    next_ref[...] = token_ref[...]
    depth = block_refs[0].shape[0]
    side = depth // 2
    e, line = pl.program_id(0), pl.program_id(1)
    total = None
    for k, block_ref in enumerate(block_refs):
        product = jnp.dot(
            dense_ref[:, k * depth : (k + 1) * depth], block_ref[...], preferred_element_type=jnp.float32
        )
        total = product if total is None else total + product
    rows = pl.ds(pl.multiple_of(e * side, side), side)
    scale_rows = pl.ds(pl.multiple_of(depth + 16 * e, 16), 16)

    @pl.when(line == 0)
    def _():
        own_ref[rows] = total

    for m, code_ref in enumerate(code_refs, 1):

        @pl.when(line == m)
        def _():
            encode(total, inverse_ref[...], code_ref, rows, scale_rows)


def terms(token, dense, inverse, blocks, rows_n):
    side = dense.shape[0] // (2 * rows_n)
    width = blocks[0].shape[1]
    whole = dense.size * 2 <= 8 * MIB
    vmem = pl.BlockSpec(memory_space=pltpu.VMEM)
    own = jax.ShapeDtypeStruct((2 * side, width), jnp.float32)
    code = jax.ShapeDtypeStruct((2 * side + 32, width), jnp.bfloat16)
    if whole and PIN_IN:
        dense = pltpu.with_memory_space_constraint(dense, pltpu.VMEM)
    if whole:
        split = dict(in_specs=[vmem] * (3 + len(blocks)), out_specs=[vmem] * (1 + rows_n))
    else:
        at_start = lambda x: pl.BlockSpec(x.shape, lambda e, m: (0, 0))
        split = dict(
            grid=(2, rows_n),
            in_specs=[
                at_start(token),
                pl.BlockSpec((side, dense.shape[1]), lambda e, m: (e * rows_n + m, 0)),
                pl.BlockSpec((side, LANES), lambda e, m: (e * rows_n + m, 0)),
            ]
            + [at_start(x) for x in blocks],
            out_specs=[at_start(token), at_start(own)] + [at_start(code)] * (rows_n - 1),
        )
    token, *out = pl.pallas_call(
        functools.partial(term_kernel if whole else term_step_kernel, len(blocks), rows_n),
        out_shape=[jax.ShapeDtypeStruct(token.shape, token.dtype), own] + [code] * (rows_n - 1),
        compiler_params=pltpu.CompilerParams(vmem_limit_bytes=(TERM_LIMIT if whole else 48) * MIB),
        cost_estimate=FREE,
        **split,
    )(token, dense, inverse, *blocks)
    return token, out


def after(token, waited):
    anywhere = pl.BlockSpec(memory_space=pl.ANY)
    vmem = pl.BlockSpec(memory_space=pltpu.VMEM)

    def kernel(token_ref, waited_ref, next_ref):
        next_ref[...] = token_ref[...]

    return pl.pallas_call(
        kernel,
        out_shape=jax.ShapeDtypeStruct(token.shape, token.dtype),
        in_specs=[vmem, anywhere],
        out_specs=vmem,
        compiler_params=pltpu.CompilerParams(vmem_limit_bytes=MIB),
        cost_estimate=FREE,
    )(token, waited)


def begin_kernel(token_ref, kept_ref, got_ref, next_ref, prior_ref, coarse_ref):
    side = kept_ref.shape[0]
    next_ref[...] = token_ref[...]
    for k, ref in enumerate((kept_ref, got_ref)):
        prior_ref[k * side : (k + 1) * side] = ref[...]
        coarse_ref[k * side : (k + 1) * side] = ref[...].astype(jnp.bfloat16)


def begin(token, kept, got):
    rows, width = 2 * kept.shape[0], kept.shape[1]
    vmem = pl.BlockSpec(memory_space=pltpu.VMEM)
    return pl.pallas_call(
        begin_kernel,
        out_shape=[
            jax.ShapeDtypeStruct(token.shape, token.dtype),
            jax.ShapeDtypeStruct((rows, width), jnp.float32),
            jax.ShapeDtypeStruct((rows, width), jnp.bfloat16),
        ],
        in_specs=[vmem] * 3,
        out_specs=[vmem] * 3,
        compiler_params=pltpu.CompilerParams(vmem_limit_bytes=UPDATE_LIMIT * MIB),
        cost_estimate=FREE,
    )(token, kept, got)


def update_kernel(count, token_ref, keep_ref, scale_ref, prior_ref, own_ref, *refs):
    code_refs, degree_refs, (next_ref, out_ref) = refs[:count], refs[count : 2 * count], refs[2 * count :]
    next_ref[...] = token_ref[...]
    depth, width = out_ref.shape
    side = depth // 2
    for e in range(2):
        rows = slice(e * side, (e + 1) * side)
        for at in range(0, width, LANES):
            lanes = slice(at, at + LANES)
            summed = own_ref[rows, lanes]
            for code_ref, degree_ref in zip(code_refs, degree_refs):
                summed += decode(code_ref, rows, depth + 16 * e, lanes) * degree_ref[rows]
            prior = prior_ref[rows, lanes]
            value = scale_ref[rows] * summed + (1.0 - spread_weight) * prior
            out_ref[rows, lanes] = jnp.where(keep_ref[rows] > 0, prior, value).astype(out_ref.dtype)


def update(token, keep, scale, prior, own, codes, degrees, dtype):
    vmem = pl.BlockSpec(memory_space=pltpu.VMEM)
    return pl.pallas_call(
        functools.partial(update_kernel, len(codes)),
        out_shape=[
            jax.ShapeDtypeStruct(token.shape, token.dtype),
            jax.ShapeDtypeStruct(prior.shape, dtype),
        ],
        in_specs=[vmem] * (5 + 2 * len(codes)),
        out_specs=[vmem] * 2,
        compiler_params=pltpu.CompilerParams(vmem_limit_bytes=2 * UPDATE_LIMIT * MIB),
        cost_estimate=FREE,
    )(token, keep, scale, prior, own, *codes, *degrees)


def columns_kernel(token_ref, labelled_ref, *refs):
    row_refs, (next_ref, keep_ref, scale_ref, *column_refs) = refs[: len(refs) // 2 - 1], refs[len(refs) // 2 - 1 :]
    next_ref[...] = token_ref[...]

    def turn(ref, out_ref):
        for k in range(out_ref.shape[0] // LANES):
            flat = jnp.broadcast_to(ref[k : k + 1], (LANES, LANES))
            out_ref[k * LANES : (k + 1) * LANES] = flat.T

    turn(labelled_ref, keep_ref)
    turn(row_refs[0], scale_ref)
    total = scale_ref[...]
    for row_ref, column_ref in zip(row_refs[1:], column_refs):
        turn(row_ref, column_ref)
        total += column_ref[...]
    scale_ref[...] = spread_weight / total


def columns(token, labelled, rows, depth):
    vmem = pl.BlockSpec(memory_space=pltpu.VMEM)
    return pl.pallas_call(
        columns_kernel,
        out_shape=[jax.ShapeDtypeStruct(token.shape, token.dtype)]
        + [jax.ShapeDtypeStruct((depth, LANES), jnp.float32)] * (1 + len(rows)),
        in_specs=[vmem] * (2 + len(rows)),
        out_specs=[vmem] * (2 + len(rows)),
        compiler_params=pltpu.CompilerParams(vmem_limit_bytes=UPDATE_LIMIT * MIB),
        cost_estimate=FREE,
    )(token, labelled, *rows)


def swap(x, axis, mask):
    size = lax.axis_size(axis)
    return lax.ppermute(x, axis, [(i, i ^ mask) for i in range(size)])


def on_device(affinity, block_rows, block_cols, block_count, labels, labelled):
    tiles = affinity[0, 0]
    rows_n = lax.axis_size("row")
    cols_n = lax.axis_size("col")
    slots, side, _ = tiles.shape
    half = labels.shape[1] // 2
    row, col = lax.axis_index("row"), lax.axis_index("col")
    core = col & 1

    count = len(PARTS)
    widths = [half * p // sum(PARTS) for p in PARTS]
    starts = [sum(widths[:i]) for i in range(count)]
    halves = []
    for s, w in zip(starts, widths):
        kept = lax.dynamic_slice_in_dim(labels, core * half + s, w, 1)
        given = lax.dynamic_slice_in_dim(labels, (1 - core) * half + s, w, 1)
        kept, given = lax.optimization_barrier((kept, given))
        halves.append((kept, swap(given, "col", 1)))

    live = jnp.arange(slots) < block_count[0, 0]
    hit = (
        ((block_rows[0, 0] ^ row)[None, None, :] == jnp.arange(rows_n)[:, None, None])
        & ((block_cols[0, 0] ^ col)[None, None, :] == jnp.arange(cols_n)[None, :, None])
        & live[None, None, :]
    )
    table = jnp.max(jnp.where(hit, jnp.arange(slots), -1), axis=2).astype(jnp.int32)
    near_tiles = swap(tiles, "col", 1)
    numbers = jnp.concatenate([table.reshape(-1), labelled])
    near_numbers = swap(numbers, "col", 1)
    near_table = near_numbers[: rows_n * cols_n].reshape(rows_n, cols_n // 2, 2)
    near_table = near_table[:, :, ::-1].reshape(rows_n, cols_n)
    table = jnp.concatenate([table, near_table], axis=1)
    both = jnp.concatenate([labelled, near_numbers[rows_n * cols_n :]])
    both = jnp.pad((both == 1).astype(jnp.float32).reshape(-1, LANES), ((0, -(2 * side // LANES) % 8), (0, 0)))
    inner = [i for i in range(cols_n) if (i >> 1) & 3 in (1, 2)]

    dense, inverse, *part = dense_tiles(table, tiles, near_tiles)
    part = [part[0]] + [swap(part[m], "row", m) for m in range(1, rows_n)]
    token = start = jnp.zeros((8, 128), jnp.float32)
    priors, held, sums, final = {}, {}, {}, {}

    def spread_out(x):
        if FORWARD:
            far = swap(x, "col", 4)
            blocks = [
                x,
                swap(x, "col", 2),
                far,
                lax.ppermute(x, "col", [(i, i ^ 6) for i in inner]),
                lax.ppermute(far, "col", [(i, i ^ 2) for i in inner]),
            ]
            if cols_n > 8:
                blocks = blocks[:3] + [blocks[3] + blocks[4]]
        else:
            blocks = [x] + [swap(x, "col", 2 * k) for k in range(1, min(4, cols_n // 2))]
        while 4 <= len(blocks) < cols_n // 2:
            blocks = blocks + [swap(b, "col", 2 * len(blocks)) for b in blocks]
        return blocks

    for name in ORDER:
        if name == "G":
            token, keep, scale, *degrees = columns(token, both, part, 2 * side)
            continue
        kind, n = name[0], int(name[1:].split(".")[0])
        c, last = n % count, n >= count * (SWEEPS - 1)
        free, token = token, (start if kind.islower() else token)
        kind = kind.upper()
        if kind == "W":
            token = after(token, held[n][int(name.split(".")[1])])
        elif kind == "A":
            token, priors[c], coarse = begin(token, *halves[c])
            held[n] = spread_out(coarse)
        elif kind == "D":
            token, (own, *codes) = terms(token, dense, inverse, held.pop(n), rows_n)
            sums[n] = own, [swap(x, "row", m) for m, x in enumerate(codes, 1)]
        else:
            dtype = jnp.float32 if last else jnp.bfloat16
            token, out = update(token, keep, scale, priors[c], *sums.pop(n), degrees, dtype)
            if last:
                final[c] = out[:side], swap(out[side:], "col", 1)
            else:
                held[n + count] = spread_out(out)
        if name[0].islower():
            token = free
    final = [final[c] for c in range(count)]
    mine, other = (jnp.concatenate([f[k] for f in final], axis=1) for k in (0, 1))
    low, high = jnp.where(core == 0, mine, other), jnp.where(core == 0, other, mine)
    return jnp.concatenate([low, high], axis=1)


def solution(mesh):
    placed = (
        P("row", "col", None, None, None),
        P("row", "col", None),
        P("row", "col", None),
        P("row", "col"),
        P(("row", "col"), None),
        P(("row", "col")),
    )
    return jax.shard_map(
        on_device, mesh=mesh, in_specs=placed, out_specs=P(("row", "col"), None), check_vma=False
    )
```
